32 devices in a mesh: wide: 8 (over y, x, core), narrow: 4 (over z).
Axes of the slice: x: 2, y: 2, z: 4, core: 2. Of those that a mesh axis runs over, the one named last changes fastest.
Arguments:
- charges: float32 [2, 64, 8192], P(None, None, ('wide', 'narrow')), may hold values from -6 to 6
- projection: float32 [64, 64], replicated, may hold values from -0.75 to 0.75
- green_hat: float32 [2, 256, 64, 512], P(None, ('wide', 'narrow')), may hold values from -6 to 6
- near_table: float32 [27, 2, 64, 64], replicated, may hold values from -0.109375 to 0.109375
- block_site: int32 [8192], P(('wide', 'narrow')), may hold values from 0 to 511, as said below
- block_count: int32 [32], P(('wide', 'narrow')), may hold values from 128 to 256, as said below
- near_source: int32 [27, 8192], P(None, ('wide', 'narrow')), may hold values from 0 to 2303
Outputs:
- result: float32 [2, 64, 8192], P(None, None, ('wide', 'narrow'))
The draws below stay inside these ranges and needn't reach their ends.
Inputs may be any that keep to these rules, and one draw needn't show every extreme that they name: `block_count`: slots at or beyond a device's count hold no block; at least one device has all 256 slots occupied. `block_site`: distinct among the slots of one device.
All inputs are finite; a program needn't handle non-finite values.
Results may differ from the reference program's by a relative error of at most 0.0003.
Values sent between devices are 32-bit elements; how exact they have to be, the bound alone decides.
A program may use at most 128 MiB of HBM per device.

```python
import jax
import jax.numpy as jnp
from jax import lax

PX = 4
PY = 64
PZ = 128
CELLS = 64
CLASSES = 27
BLOCK_SLOTS = 256
RANKS = 32
BLOCKS = 8192
GX = 64
GY = 512
GZ = 256
N_WIDE = 8
N_NARROW = 4


def draw_block_site(key, part):
    key = jax.random.fold_in(key, 11)
    device_keys = jax.random.split(key, RANKS)
    lattice = PX // 4 * (PY // 4) * (PZ // 4)

    def choose_sites(single):
        return jax.random.permutation(single, lattice)[:BLOCK_SLOTS]
    chosen = jax.vmap(choose_sites)(device_keys)
    return chosen.reshape(RANKS * BLOCK_SLOTS).astype(jnp.int32)


def draw_block_count(key, part):
    key = jax.random.fold_in(key, 23)
    count_key, full_key = jax.random.split(key)
    counts = jax.random.randint(count_key, (RANKS,), BLOCK_SLOTS // 2, BLOCK_SLOTS + 1)
    fullest = jax.random.randint(full_key, (), 0, RANKS)
    return jnp.where(jnp.arange(RANKS) == fullest, BLOCK_SLOTS, counts).astype(jnp.int32)


def set_ends(drawn, own_key, smallest, largest):
    shape = drawn.shape
    place = [jax.random.randint(jax.random.fold_in(own_key, axis), (), 0, shape[axis]) for axis in range(len(shape))]
    drawn = drawn.at[tuple(place)].set(smallest)
    longest = shape.index(max(shape))
    place[longest] = (place[longest] + 1) % shape[longest]
    return drawn.at[tuple(place)].set(largest)


def block_scale(own_key, shape, shards, least, high):
    factor_of, own = 1.0, jax.random.fold_in(own_key, 6)
    for dim, parts in shards:
        draws = jnp.exp(jax.random.uniform(jax.random.fold_in(own, dim), (parts,), jnp.float32, least / len(shards), high / len(shards)))
        factor_of = factor_of * jnp.repeat(draws, shape[dim] // parts).reshape([-1 if axis == dim else 1 for axis in range(len(shape))])
    return factor_of


def gaussian(stream_key, extent, scale, most, pieces=(), kind=jnp.bfloat16):
    drawn = jax.random.normal(stream_key, extent, jnp.float32) * scale
    if len(pieces) > 0:
        drawn = block_scale(stream_key, extent, pieces, -0.22, 0.18) * drawn
    return jnp.clip(drawn, min=-most, max=most).astype(kind)


def setup_inputs(seed: int = 0) -> dict:
    seeds = jax.random.split(jax.random.key(seed), 8)
    return {
        "charges": gaussian(seeds[0], (2, CELLS, BLOCKS), 1.0, 6.0, ((2, 32),), jnp.float32),
        "projection": gaussian(seeds[1], (CELLS, CELLS), CELLS ** -0.5, 0.75, (), jnp.float32),
        "green_hat": gaussian(seeds[2], (2, GZ, GX, GY), 1.0, 6.0, ((1, 32),), jnp.float32),
        "near_table": gaussian(seeds[3], (CLASSES, 2, CELLS, CELLS), (2 * CLASSES * CELLS) ** -0.5, 0.109375, (), jnp.float32),
        "block_site": draw_block_site(jax.random.fold_in(seeds[7], 71), 0),
        "block_count": draw_block_count(jax.random.fold_in(seeds[7], 71), 0),
        "near_source": set_ends(jax.random.randint(seeds[6], (CLASSES, BLOCKS), 0, 9 * BLOCK_SLOTS), jax.random.fold_in(seeds[6], 1), 0, (9 * BLOCK_SLOTS) - 1).astype(jnp.int32),
    }


EXACT = lax.Precision.HIGHEST


def reference(charges, projection, green_hat, near_table, block_site, block_count, near_source):
    span_x = PX // 4
    span_y = PY // 4
    span_z = PZ // 4
    lattice = span_x * span_y * span_z
    owners = jnp.arange(BLOCKS, dtype=jnp.int32) // BLOCK_SLOTS
    slot_index = jnp.arange(BLOCKS, dtype=jnp.int32) % BLOCK_SLOTS
    occupied = (slot_index < block_count[owners]).astype(jnp.float32)
    masked = charges * occupied
    stencil = jnp.einsum('gc,rcb->rgb', projection, masked, precision=EXACT, preferred_element_type=jnp.float32)
    position = owners * lattice + block_site
    placed = jnp.zeros((2, CELLS, RANKS * lattice), jnp.float32).at[:, :, position].add(stencil)
    grid_field = placed.reshape(2, 4, 4, 4, N_WIDE, N_NARROW, span_x, span_y, span_z)
    grid_field = grid_field.transpose(0, 4, 6, 1, 5, 7, 2, 8, 3).reshape(2, GX // 2, GY // 2, PZ)
    widths = ((0, GX // 2), (0, GY // 2), (0, GZ - PZ))
    complex_grid = jnp.pad(grid_field[0], widths) + 1j * jnp.pad(grid_field[1], widths)
    spectrum = jnp.fft.fftn(complex_grid)
    kernel = (green_hat[0] + 1j * green_hat[1]).transpose(1, 2, 0)
    potential = jnp.fft.ifftn(spectrum * kernel)[: GX // 2, : GY // 2, :PZ]
    values = jnp.stack([jnp.real(potential), jnp.imag(potential)])
    blocks = values.reshape(2, N_WIDE, span_x, 4, N_NARROW, span_y, 4, span_z, 4)
    blocks = blocks.transpose(0, 3, 6, 8, 1, 4, 2, 5, 7).reshape(2, CELLS, RANKS * lattice)
    gathered = blocks[:, :, position] * occupied
    far_field = jnp.einsum('gc,rgb->rcb', projection, gathered, precision=EXACT, preferred_element_type=jnp.float32)
    padded_cube = jnp.pad(masked.reshape(2, CELLS, N_WIDE, N_NARROW, BLOCK_SLOTS), ((0, 0), (0, 0), (1, 1), (1, 1), (0, 0)))
    padded_cube = padded_cube.reshape(2, CELLS, (N_WIDE + 2) * (N_NARROW + 2) * BLOCK_SLOTS)
    wide_pos = owners // N_NARROW
    narrow_pos = owners % N_NARROW

    def one_class(running, inputs):
        matrix, source = inputs
        step_wide = source // (3 * BLOCK_SLOTS)
        step_narrow = (source // BLOCK_SLOTS) % 3
        slot_pick = source % BLOCK_SLOTS
        flat_index = ((wide_pos + step_wide) * (N_NARROW + 2) + narrow_pos + step_narrow) * BLOCK_SLOTS + slot_pick
        picked = padded_cube[:, :, flat_index]
        real_part = jnp.dot(matrix[0], picked[0], precision=EXACT, preferred_element_type=jnp.float32) - jnp.dot(matrix[1], picked[1], precision=EXACT, preferred_element_type=jnp.float32)
        imag_part = jnp.dot(matrix[0], picked[1], precision=EXACT, preferred_element_type=jnp.float32) + jnp.dot(matrix[1], picked[0], precision=EXACT, preferred_element_type=jnp.float32)
        return running + jnp.stack([real_part, imag_part]), None

    near_field, _ = lax.scan(one_class, jnp.zeros((2, CELLS, BLOCKS), jnp.float32), (near_table, near_source))
    return far_field + near_field * occupied
```

```python
import functools

import jax
import jax.numpy as jnp
import ml_dtypes
import numpy as np
from jax import lax
from jax.experimental import pallas as pl
from jax.experimental.pallas import tpu as pltpu
from jax.sharding import PartitionSpec as P

PX = 4
PY = 64
PZ = 128
SPAN_Y = PY // 4
SPAN_Z = PZ // 4
ROW = 2 * PY
WIDTH = PX * ROW
VMEM_LIMIT = 48 * 1024 * 1024
F32 = jnp.float32
BF16 = jnp.bfloat16


def halves(table):
    high = table.astype(np.float32).astype(ml_dtypes.bfloat16)
    low = (table - high.astype(np.float64)).astype(np.float32).astype(ml_dtypes.bfloat16)
    return high, low


def waves(left, right, length):
    angles = 2.0 * np.pi * (np.outer(left, right) % length) / length
    return np.cos(angles), np.sin(angles)


@functools.lru_cache(maxsize=None)
def constant_tables(wide_count, narrow_count):
    whole_x = 2 * PX * wide_count
    whole_y = 2 * PY * narrow_count
    whole_z = 2 * PZ
    ez, ex, part, ey, _ = np.unravel_index(
        np.arange(4 * WIDTH), (4, PX, 2, 4, SPAN_Y)
    )
    owner = part * 64 + 16 * ex + 4 * ey + ez
    spread = (np.arange(128)[:, None] == owner[None, :]).astype(ml_dtypes.bfloat16)
    depth = (4 * np.arange(SPAN_Z)[None, :] + np.arange(4)[:, None]).reshape(-1)
    cos_z, sin_z = waves(np.arange(whole_z), depth, whole_z)
    forward_z = np.concatenate([cos_z, sin_z], axis=1)
    inverse_z = np.concatenate([cos_z.T, sin_z.T], axis=1) / (whole_x * whole_y * whole_z)
    line = (4 * np.arange(SPAN_Y)[None, :] + np.arange(4)[:, None]).reshape(-1)
    points = (PY * np.arange(narrow_count)[:, None] + line[None, :]).reshape(-1)
    cos_y, sin_y = waves(points, np.arange(whole_y), whole_y)
    real_rows = np.concatenate([cos_y, -sin_y], axis=1).reshape(narrow_count, 1, PY, 2 * whole_y)
    imag_rows = np.concatenate([sin_y, cos_y], axis=1).reshape(narrow_count, 1, PY, 2 * whole_y)
    forward_y = np.concatenate([real_rows, imag_rows], axis=1).reshape(-1, 2 * whole_y)
    cos_x, sin_x = waves(np.arange(whole_x), np.arange(whole_x // 2), whole_x)
    forward_x = np.block([[cos_x, sin_x], [-sin_x, cos_x]])
    packed = []
    for table in (forward_x, forward_x.T):
        high, low = halves(table)
        packed.append(np.concatenate([high, high, low], axis=1))
    return {
        "spread": spread,
        "gather": np.ascontiguousarray(spread.T),
        "forward_z": halves(forward_z),
        "inverse_z": halves(inverse_z),
        "forward_y": halves(forward_y),
        "inverse_y": halves(np.ascontiguousarray(forward_y.T)),
        "forward_x": packed[0],
        "inverse_x": packed[1],
    }


def split(values):
    high = values.astype(BF16)
    return high, (values - high.astype(F32)).astype(BF16)


def dot(left, right, dims=((1,), (0,))):
    return lax.dot_general(left, right, (dims, ((), ())), preferred_element_type=F32)


def dot3(left, right, dims=((1,), (0,))):
    lh, ll = left
    rh, rl = right
    return dot(lh, rh, dims) + (dot(ll, rh, dims) + dot(lh, rl, dims))


def turned(values, sign):
    lanes = lax.broadcasted_iota(jnp.int32, (values.shape[0], ROW), 1)
    factor = jnp.where(lanes < PY, sign, -sign).astype(F32)
    pieces = [
        pltpu.roll(values[:, i * ROW : (i + 1) * ROW], PY, 1) * factor
        for i in range(values.shape[1] // ROW)
    ]
    return jnp.concatenate(pieces, axis=1)


def columns_of(row, slots):
    return jnp.broadcast_to(row.astype(F32), (128, slots)).T


def own_line(site, slots):
    line = columns_of(site // SPAN_Z, slots)
    lanes = lax.broadcasted_iota(jnp.int32, (slots, 128), 1) % SPAN_Y
    match = line == lanes.astype(F32)
    return jnp.concatenate([match.astype(F32)] * (WIDTH // 128), axis=1)


def place_kernel(count, charges, projection, site, spread, zh, zl, masked_out, send):
    slots = charges.shape[2]
    slot = lax.broadcasted_iota(jnp.int32, (1, slots), 1)
    occupied = (slot < count[0]).astype(F32)
    parts = [charges[r] * occupied for r in range(2)]
    masked_out[...] = jnp.concatenate(parts, axis=0).T
    weights = split(projection[...])
    stencil = jnp.concatenate([dot3(weights, split(p)) for p in parts], axis=0).T
    high, low = split(stencil)
    table = spread[...]
    spread_out = dot(
        jnp.concatenate([high, low], axis=1), jnp.concatenate([table, table], axis=0)
    )
    mask = own_line(site[...], slots)
    depth = lax.broadcasted_iota(jnp.int32, (SPAN_Z, slots), 0)
    picker = (depth == site[...] % SPAN_Z).astype(F32).astype(BF16)
    rows = []
    for ez in range(4):
        high, low = split(spread_out[:, ez * WIDTH : (ez + 1) * WIDTH] * mask)
        rows.append(dot(picker, high) + dot(picker, low))
    grid = jnp.concatenate(rows, axis=0)
    both = jnp.concatenate([grid, turned(grid, 1.0)], axis=0)
    freq = dot3((zh[...], zl[...]), split(both))
    planes = send.shape[1] // PX
    for ex in range(PX):
        block = freq[:, ex * ROW : (ex + 1) * ROW]
        send[:, ex * planes : (ex + 1) * planes, :] = block.reshape(send.shape[0], planes, ROW)


def plane_kernel(wide, narrow, recv, green, fyh, fyl, iyh, iyl, fx, ix, send, lines, back):
    planes = green.shape[1]
    whole_x, whole_y = green.shape[2:]
    half_x = whole_x // 2
    group = recv.shape[1]
    chunks = 2 * whole_y // 128
    values = recv[...].reshape(wide, narrow, group, ROW)
    field = jnp.concatenate(
        [values[:, n].reshape(wide * group, ROW) for n in range(narrow)], axis=1
    )
    freq = dot3(split(field), (fyh[...], fyl[...]))
    for c in range(chunks):
        lines[c] = freq[:, c * 128 : (c + 1) * 128]
    for z in range(planes):
        at = pl.ds(z, half_x, stride=planes) if planes > 1 else pl.ds(0, half_x)
        taken = [lines[c, at, :] for c in range(chunks)]
        column = jnp.concatenate(
            [
                jnp.concatenate(taken[: chunks // 2], axis=1),
                jnp.concatenate(taken[chunks // 2 :], axis=1),
            ],
            axis=0,
        )
        high, low = split(column)
        freq = dot(fx[...], jnp.concatenate([high, low, high], axis=0))
        real, imag = freq[:whole_x], freq[whole_x:]
        gr, gi = green[0, z], green[1, z]
        product = jnp.concatenate([gr * real - gi * imag, gr * imag + gi * real], axis=0)
        high, low = split(product)
        column = dot(ix[...], jnp.concatenate([high, low, high], axis=0))
        for c in range(chunks):
            part, lane = divmod(c, chunks // 2)
            back[c, at, :] = column[
                part * half_x : (part + 1) * half_x, lane * 128 : (lane + 1) * 128
            ]
    field = jnp.concatenate([back[c] for c in range(chunks)], axis=1)
    out = dot3(split(field), (iyh[...], iyl[...]))
    for n in range(narrow):
        block = out[:, n * ROW : (n + 1) * ROW].reshape(wide, group, ROW)
        for w in range(wide):
            send[w * narrow + n] = block[w]


def near_kernel(source, before, own, after, table, near, cube, picked):
    third = own.shape[0]
    cube[:third] = before[...]
    cube[third : 2 * third] = own[...]
    cube[2 * third :] = after[...]
    classes, slots = source.shape
    near[...] = jnp.zeros(near.shape, F32)

    def one_class(k, carry):
        def eight(i, inner):
            base = pl.multiple_of(i * 16, 16)
            for j in range(16):
                picked[pl.ds(base + j, 1), :] = cube[pl.ds(source[k, base + j], 1), :]
            return inner

        lax.fori_loop(0, slots // 16, eight, 0)
        real, imag = table[k, 0], table[k, 1]
        matrix = jnp.concatenate(
            [
                jnp.concatenate([real, -imag], axis=1),
                jnp.concatenate([imag, real], axis=1),
            ],
            axis=0,
        )
        near[...] += dot3(split(picked[...]), split(matrix), ((1,), (1,)))
        return carry

    lax.fori_loop(0, classes, one_class, 0)


def finish_kernel(count, recv, projection, site, gather, zh, zl, near, out):
    slots = out.shape[2]
    planes = recv.shape[1] // PX
    freq = jnp.concatenate(
        [
            recv[:, ex * planes : (ex + 1) * planes, :].reshape(recv.shape[0] * planes, ROW)
            for ex in range(PX)
        ],
        axis=1,
    )
    both = jnp.concatenate([freq, turned(freq, -1.0)], axis=0)
    grid = dot3((zh[...], zl[...]), split(both))
    mask = own_line(site[...], slots)
    depth = lax.broadcasted_iota(jnp.int32, (slots, 128), 1)
    match = columns_of(site[...] % SPAN_Z, slots) == depth.astype(F32)
    picker = match.astype(F32).astype(BF16)[:, :SPAN_Z]
    total = jnp.zeros((slots, 128), F32)
    for ez in range(4):
        high, low = split(grid[ez * SPAN_Z : (ez + 1) * SPAN_Z])
        taken = (dot(picker, high) + dot(picker, low)) * mask
        high, low = split(taken)
        table = gather[ez * WIDTH : (ez + 1) * WIDTH, :]
        total = total + (dot(high, table) + dot(low, table))
    taken = total.T
    beside = near[...].T
    weights = split(projection[...])
    slot = lax.broadcasted_iota(jnp.int32, (1, slots), 1)
    occupied = (slot < count[0]).astype(F32)
    cells = out.shape[1]
    for r in range(2):
        far = dot3(weights, split(taken[r * 64 : (r + 1) * 64]), ((0,), (0,)))
        out[r] = (far + beside[r * cells : (r + 1) * cells]) * occupied


def call(kernel, out_shape, operands, scratch=(), scalars=(), flops=0, moved=0):
    spaces = [
        pl.BlockSpec(memory_space=pltpu.SMEM if i in scalars else pltpu.VMEM)
        for i in range(len(operands))
    ]
    outs = jax.tree.map(lambda _: pl.BlockSpec(memory_space=pltpu.VMEM), out_shape)
    return pl.pallas_call(
        kernel,
        out_shape=out_shape,
        in_specs=spaces,
        out_specs=outs,
        scratch_shapes=list(scratch),
        compiler_params=pltpu.CompilerParams(vmem_limit_bytes=VMEM_LIMIT),
        cost_estimate=pl.CostEstimate(flops=flops, bytes_accessed=moved, transcendentals=0),
    )(*operands)


def shifted(array, axis, step):
    devices = lax.axis_size(axis)
    pairs = [(i, i + step) for i in range(devices) if 0 <= i + step < devices]
    return lax.ppermute(array, axis, pairs)


def per_device(charges, projection, green_hat, near_table, block_site, block_count, near_source):
    wide = lax.axis_size("wide")
    narrow = lax.axis_size("narrow")
    tables = constant_tables(wide, narrow)
    cells, slots = charges.shape[1:]
    planes = green_hat.shape[1]
    whole_x, whole_y = green_hat.shape[2:]
    site = block_site.reshape(1, slots)
    block = jax.ShapeDtypeStruct((wide * narrow, PX * planes, ROW), F32)
    masked, send = call(
        place_kernel,
        (jax.ShapeDtypeStruct((slots, 2 * cells), F32), block),
        (block_count, charges, projection, site, tables["spread"], *tables["forward_z"]),
        scalars=(0,),
        flops=10**9,
        moved=3 * 10**6,
    )
    recv = lax.all_to_all(send, ("wide", "narrow"), 0, 0, tiled=True)
    own = jnp.concatenate(
        [shifted(masked, "narrow", 1), masked, shifted(masked, "narrow", -1)], axis=0
    )
    before, after = shifted(own, "wide", 1), shifted(own, "wide", -1)
    near = call(
        near_kernel,
        jax.ShapeDtypeStruct((slots, 2 * cells), F32),
        (near_source, before, own, after, near_table),
        scratch=(
            pltpu.VMEM((9 * slots, 2 * cells), F32),
            pltpu.VMEM((slots, 2 * cells), F32),
        ),
        scalars=(0,),
        flops=10**10,
        moved=10**7,
    )
    lines = pltpu.VMEM((2 * whole_y // 128, whole_x // 2 * planes, 128), F32)
    send = call(
        functools.partial(plane_kernel, wide, narrow),
        block,
        (
            recv,
            green_hat,
            *tables["forward_y"],
            *tables["inverse_y"],
            tables["forward_x"],
            tables["inverse_x"],
        ),
        scratch=(lines, lines),
        flops=3 * 10**9,
        moved=9 * 10**6,
    )
    recv = lax.all_to_all(send, ("wide", "narrow"), 0, 0, tiled=True)
    return call(
        finish_kernel,
        jax.ShapeDtypeStruct((2, cells, slots), F32),
        (
            block_count,
            recv,
            projection,
            site,
            tables["gather"],
            *tables["inverse_z"],
            near,
        ),
        scalars=(0,),
        flops=10**9,
        moved=3 * 10**6,
    )


def solution(mesh):
    placed = (
        P(None, None, ("wide", "narrow")),
        P(),
        P(None, ("wide", "narrow"), None, None),
        P(),
        P(("wide", "narrow")),
        P(("wide", "narrow")),
        P(None, ("wide", "narrow")),
    )
    return jax.shard_map(
        per_device,
        mesh=mesh,
        in_specs=placed,
        out_specs=P(None, None, ("wide", "narrow")),
        check_vma=False,
    )
```

```python
import functools

import jax
import jax.numpy as jnp
import ml_dtypes
import numpy as np
from jax import lax
from jax.experimental import pallas as pl
from jax.experimental.pallas import tpu as pltpu
from jax.sharding import PartitionSpec as P

PX = 4
PY = 64
PZ = 128
SPAN_Y = PY // 4
SPAN_Z = PZ // 4
ROW = 2 * PY
WIDTH = PX * ROW
VMEM_LIMIT = 56 * 1024 * 1024
CLOSE = 9
F32 = jnp.float32
BF16 = jnp.bfloat16


def halves(table):
    high = table.astype(np.float32).astype(ml_dtypes.bfloat16)
    low = (table - high.astype(np.float64)).astype(np.float32).astype(ml_dtypes.bfloat16)
    return high, low


def waves(left, right, length):
    angles = 2.0 * np.pi * (np.outer(left, right) % length) / length
    return np.cos(angles), np.sin(angles)


@functools.lru_cache(maxsize=None)
def constant_tables(wide_count, narrow_count):
    whole_x = 2 * PX * wide_count
    whole_y = 2 * PY * narrow_count
    whole_z = 2 * PZ
    ez, ex, part, ey, _ = np.unravel_index(
        np.arange(4 * WIDTH), (4, PX, 2, 4, SPAN_Y)
    )
    owner = part * 64 + 16 * ex + 4 * ey + ez
    spread = (np.arange(128)[:, None] == owner[None, :]).astype(ml_dtypes.bfloat16)
    depth = (4 * np.arange(SPAN_Z)[None, :] + np.arange(4)[:, None]).reshape(-1)
    cos_z, sin_z = waves(np.arange(whole_z), depth, whole_z)
    forward_z = np.concatenate([cos_z, sin_z], axis=1)
    inverse_z = np.concatenate([cos_z.T, sin_z.T], axis=1) / (whole_x * whole_y * whole_z)
    line = (4 * np.arange(SPAN_Y)[None, :] + np.arange(4)[:, None]).reshape(-1)
    points = (PY * np.arange(narrow_count)[:, None] + line[None, :]).reshape(-1)
    cos_y, sin_y = waves(points, np.arange(whole_y), whole_y)
    real_rows = np.concatenate([cos_y, -sin_y], axis=1).reshape(narrow_count, 1, PY, 2 * whole_y)
    imag_rows = np.concatenate([sin_y, cos_y], axis=1).reshape(narrow_count, 1, PY, 2 * whole_y)
    forward_y = np.concatenate([real_rows, imag_rows], axis=1).reshape(-1, 2 * whole_y)
    cos_x, sin_x = waves(np.arange(whole_x), np.arange(whole_x // 2), whole_x)
    forward_x = np.block([[cos_x, sin_x], [-sin_x, cos_x]])
    packed = []
    for table in (forward_x, forward_x.T):
        high, low = halves(table)
        packed.append(np.concatenate([high, high, low], axis=1))
    return {
        "spread": spread,
        "gather": np.ascontiguousarray(spread.T),
        "forward_z": halves(forward_z),
        "inverse_z": halves(inverse_z),
        "forward_y": halves(forward_y),
        "inverse_y": halves(np.ascontiguousarray(forward_y.T)),
        "forward_x": packed[0],
        "inverse_x": packed[1],
    }


def split(values):
    high = values.astype(BF16)
    return high, (values - high.astype(F32)).astype(BF16)


def dot(left, right, dims=((1,), (0,))):
    return lax.dot_general(left, right, (dims, ((), ())), preferred_element_type=F32)


def dot3(left, right, dims=((1,), (0,))):
    lh, ll = left
    rh, rl = right
    return dot(lh, rh, dims) + (dot(ll, rh, dims) + dot(lh, rl, dims))


def turned(values, sign):
    lanes = lax.broadcasted_iota(jnp.int32, (values.shape[0], ROW), 1)
    factor = jnp.where(lanes < PY, sign, -sign).astype(F32)
    pieces = [
        pltpu.roll(values[:, i * ROW : (i + 1) * ROW], PY, 1) * factor
        for i in range(values.shape[1] // ROW)
    ]
    return jnp.concatenate(pieces, axis=1)


def columns_of(row, slots):
    return jnp.broadcast_to(row.astype(F32), (128, slots)).T


def own_line(site, slots):
    line = columns_of(site // SPAN_Z, slots)
    lanes = lax.broadcasted_iota(jnp.int32, (slots, 128), 1) % SPAN_Y
    match = line == lanes.astype(F32)
    return jnp.concatenate([match.astype(F32)] * (WIDTH // 128), axis=1)


def place(masked, projection, site, table):
    slots = masked.shape[1]
    cells = masked.shape[0] // 2
    weights = split(projection)
    stencil = jnp.concatenate(
        [dot3(weights, split(masked[r * cells : (r + 1) * cells])) for r in range(2)], axis=0
    ).T
    high, low = split(stencil)
    spread = dot(jnp.concatenate([high, low], axis=1), jnp.concatenate([table, table], axis=0))
    mask = own_line(site, slots)
    depth = lax.broadcasted_iota(jnp.int32, (SPAN_Z, slots), 0)
    picker = (depth == site % SPAN_Z).astype(F32).astype(BF16)
    rows = []
    for ez in range(4):
        high, low = split(spread[:, ez * WIDTH : (ez + 1) * WIDTH] * mask)
        rows.append(dot(picker, high) + dot(picker, low))
    grid = jnp.concatenate(rows, axis=0)
    return jnp.concatenate([grid, turned(grid, 1.0)], axis=0)


def gather_points(grid, site, slots, table):
    mask = own_line(site, slots)
    depth = lax.broadcasted_iota(jnp.int32, (slots, 128), 1)
    match = columns_of(site % SPAN_Z, slots) == depth.astype(F32)
    picker = match.astype(F32).astype(BF16)[:, :SPAN_Z]
    total = jnp.zeros((slots, 128), F32)
    for ez in range(4):
        high, low = split(grid[ez * SPAN_Z : (ez + 1) * SPAN_Z])
        taken = (dot(picker, high) + dot(picker, low)) * mask
        high, low = split(taken)
        rows = table[ez * WIDTH : (ez + 1) * WIDTH, :]
        total = total + (dot(high, rows) + dot(low, rows))
    return total.T


def plane_transforms(z, lines, back, green, fx, ix, planes):
    whole_x = green.shape[2]
    half_x = whole_x // 2
    chunks = lines.shape[0]
    at = pl.ds(z, half_x, stride=planes) if planes > 1 else pl.ds(0, half_x)
    taken = [lines[c, at, :] for c in range(chunks)]
    column = jnp.concatenate(
        [
            jnp.concatenate(taken[: chunks // 2], axis=1),
            jnp.concatenate(taken[chunks // 2 :], axis=1),
        ],
        axis=0,
    )
    high, low = split(column)
    freq = dot(fx[...], jnp.concatenate([high, low, high], axis=0))
    real, imag = freq[:whole_x], freq[whole_x:]
    gr, gi = green[0, z], green[1, z]
    product = jnp.concatenate([gr * real - gi * imag, gr * imag + gi * real], axis=0)
    high, low = split(product)
    column = dot(ix[...], jnp.concatenate([high, low, high], axis=0))
    for c in range(chunks):
        part, lane = divmod(c, chunks // 2)
        back[c, at, :] = column[
            part * half_x : (part + 1) * half_x, lane * 128 : (lane + 1) * 128
        ]


def near_class(k, source, table, close):
    slots = source.shape[1]
    row = source[pl.ds(k, 1), :]
    slot = lax.broadcasted_iota(jnp.int32, (slots, slots), 0)
    onehot = (slot == row % slots).astype(F32).astype(BF16)
    block = row // slots
    height = close.shape[0] // CLOSE
    picked = jnp.zeros((height, slots), F32)
    for i in range(CLOSE):
        some = dot(close[i * height : (i + 1) * height, :], onehot)
        picked = jnp.where(block == i, some, picked)
    picked = picked.astype(BF16)
    real, imag = table[k, 0], table[k, 1]
    matrix = jnp.concatenate(
        [jnp.concatenate([real, -imag], axis=1), jnp.concatenate([imag, real], axis=1)],
        axis=0,
    )
    high, low = split(matrix)
    return dot(jnp.concatenate([high, high], axis=1), picked) + dot(low, picked[: height // 2])


def operator_kernel(wide, narrow, loads, *refs):
    count, charges, projection, site, source = refs[:5]
    far_refs = refs[5 : 5 + loads]
    out = refs[5 + loads]
    held = refs[6 + loads : 6 + 2 * loads]
    (
        send_a, recv_a, send_b, recv_b, lines, back, cube, close, near,
        load_sem, send_sem_a, recv_sem_a, send_sem_b, recv_sem_b, halo_send, halo_recv,
    ) = refs[6 + 2 * loads :]
    spread, fzh, fzl, fyh, fyl, fx, green, ix, iyh, iyl, near_table, izh, izl, gather = held
    devices = wide * narrow
    w, n = lax.axis_index("wide"), lax.axis_index("narrow")
    me = w * narrow + n
    _, cells, slots = charges.shape
    planes = green.shape[1]
    chunks = lines.shape[0]
    group = PX * planes

    barrier = pltpu.get_barrier_semaphore()

    def place_of(step):
        to = lax.rem(me + step, devices)
        return to, (lax.div(to, narrow), lax.rem(to, narrow))

    def greet(step, carry):
        pl.semaphore_signal(
            barrier, inc=1, device_id=place_of(step)[1], device_id_type=pl.DeviceIdType.MESH
        )
        return carry

    lax.fori_loop(1, devices, greet, 0)
    copies = [
        pltpu.make_async_copy(far_refs[i], held[i], load_sem.at[i]) for i in range(loads)
    ]
    for copy in copies:
        copy.start()

    def exchange(step, send, recv, send_sem, recv_sem):
        to, device = place_of(step)
        return pltpu.make_async_remote_copy(
            src_ref=send.at[to],
            dst_ref=recv.at[me],
            send_sem=send_sem.at[step],
            recv_sem=recv_sem.at[step],
            device_id=device,
            device_id_type=pl.DeviceIdType.MESH,
        )

    def start_all(*buffers):
        def one(step, carry):
            exchange(step, *buffers).start()
            return carry

        lax.fori_loop(1, devices, one, 0)

    def receive_all(*buffers):
        def one(step, carry):
            exchange(step, *buffers).wait_recv()
            return carry

        lax.fori_loop(1, devices, one, 0)

    def sent_all(*buffers):
        def one(step, carry):
            exchange(step, *buffers).wait_send()
            return carry

        lax.fori_loop(1, devices, one, 0)

    def beside(index, src, dst, device):
        return pltpu.make_async_remote_copy(
            src_ref=src,
            dst_ref=dst,
            send_sem=halo_send.at[index],
            recv_sem=halo_recv.at[index],
            device_id=device,
            device_id_type=pl.DeviceIdType.MESH,
        )

    narrow_halo = (
        (n < narrow - 1, n > 0, beside(0, cube.at[4], cube.at[3], (w, n + 1))),
        (n > 0, n < narrow - 1, beside(1, cube.at[4], cube.at[5], (w, n - 1))),
    )
    wide_halo = (
        (w < wide - 1, w > 0, beside(2, cube.at[3:6], cube.at[0:3], (w + 1, n))),
        (w > 0, w < wide - 1, beside(3, cube.at[3:6], cube.at[6:9], (w - 1, n))),
    )

    def start_halo(halo):
        for sends, _, copy in halo:
            pl.when(sends)(copy.start)

    def receive_halo(halo):
        for _, receives, copy in halo:
            pl.when(receives)(copy.wait_recv)

    def sent_halo(halo):
        for sends, _, copy in halo:
            pl.when(sends)(copy.wait_send)

    for outside, blocks in (
        (n == 0, (3, 4)),
        (n == narrow - 1, (5, 6)),
        (w == 0, (0, 3)),
        (w == wide - 1, (6, 9)),
    ):

        @pl.when(outside)
        def _(blocks=blocks):
            for i in range(*blocks):
                cube[i] = jnp.zeros(cube.shape[1:], F32)

    slot = lax.broadcasted_iota(jnp.int32, (1, slots), 1)
    occupied = (slot < count[0]).astype(F32)
    masked = jnp.concatenate([charges[r] * occupied for r in range(2)], axis=0)
    cube[4] = masked
    copies[0].wait()
    grid = place(masked, projection[...], site[...], spread[...])
    copies[1].wait()
    copies[2].wait()
    freq = dot3((fzh[...], fzl[...]), split(grid))
    for ex in range(PX):
        block = freq[:, ex * ROW : (ex + 1) * ROW]
        send_a[:, ex * planes : (ex + 1) * planes, :] = block.reshape(devices, planes, ROW)

    pl.semaphore_wait(barrier, devices - 1)
    first = (send_a, recv_a, send_sem_a, recv_sem_a)
    start_all(*first)
    start_halo(narrow_halo)
    recv_a[pl.ds(me, 1)] = send_a[pl.ds(me, 1)]
    for copy in copies[3:]:
        copy.wait()
    receive_all(*first)

    values = recv_a[...].reshape(wide, narrow, group, ROW)
    field = jnp.concatenate(
        [values[:, i].reshape(wide * group, ROW) for i in range(narrow)], axis=1
    )
    freq = dot3(split(field), (fyh[...], fyl[...]))
    for c in range(chunks):
        lines[c] = freq[:, c * 128 : (c + 1) * 128]
    receive_halo(narrow_halo)
    start_halo(wide_halo)
    for z in range(planes):
        plane_transforms(z, lines, back, green, fx, ix, planes)
    field = jnp.concatenate([back[c] for c in range(chunks)], axis=1)
    result = dot3(split(field), (iyh[...], iyl[...]))
    for i in range(narrow):
        block = result[:, i * ROW : (i + 1) * ROW].reshape(wide, group, ROW)
        for j in range(wide):
            send_b[j * narrow + i] = block[j]
    second = (send_b, recv_b, send_sem_b, recv_sem_b)
    start_all(*second)
    recv_b[pl.ds(me, 1)] = send_b[pl.ds(me, 1)]

    receive_halo(wide_halo)
    rows = 2 * cells
    for i in range(CLOSE):
        high, low = split(cube[i])
        close[2 * i * rows : (2 * i + 1) * rows, :] = high
        close[(2 * i + 1) * rows : (2 * i + 2) * rows, :] = low
    near[...] = jnp.zeros(near.shape, F32)

    def one_class(k, carry):
        near[...] += near_class(k, source, near_table, close)
        return carry

    lax.fori_loop(0, source.shape[0], one_class, 0)

    receive_all(*second)
    freq = jnp.concatenate(
        [
            recv_b[:, ex * planes : (ex + 1) * planes, :].reshape(devices * planes, ROW)
            for ex in range(PX)
        ],
        axis=1,
    )
    both = jnp.concatenate([freq, turned(freq, -1.0)], axis=0)
    grid = dot3((izh[...], izl[...]), split(both))
    taken = gather_points(grid, site[...], slots, gather)
    weights = split(projection[...])
    for r in range(2):
        far = dot3(weights, split(taken[r * 64 : (r + 1) * 64]), ((0,), (0,)))
        out[r] = (far + near[r * cells : (r + 1) * cells, :]) * occupied
    sent_all(*first)
    sent_all(*second)
    sent_halo(narrow_halo)
    sent_halo(wide_halo)


def per_device(charges, projection, green_hat, near_table, block_site, block_count, near_source):
    wide = lax.axis_size("wide")
    narrow = lax.axis_size("narrow")
    devices = wide * narrow
    tables = constant_tables(wide, narrow)
    cells, slots = charges.shape[1:]
    planes = green_hat.shape[1]
    whole_x, whole_y = green_hat.shape[2:]
    loaded = (
        tables["spread"],
        *tables["forward_z"],
        *tables["forward_y"],
        tables["forward_x"],
        green_hat,
        tables["inverse_x"],
        *tables["inverse_y"],
        near_table,
        *tables["inverse_z"],
        tables["gather"],
    )
    block = pltpu.VMEM((devices, PX * planes, ROW), F32)
    lines = pltpu.VMEM((2 * whole_y // 128, whole_x // 2 * planes, 128), F32)
    one = pltpu.SemaphoreType.DMA((devices,))
    halo = pltpu.SemaphoreType.DMA((4,))
    vmem = pl.BlockSpec(memory_space=pltpu.VMEM)
    return pl.pallas_call(
        functools.partial(operator_kernel, wide, narrow, len(loaded)),
        out_shape=jax.ShapeDtypeStruct((2, cells, slots), F32),
        in_specs=[pl.BlockSpec(memory_space=pltpu.SMEM)]
        + [vmem] * 4
        + [pl.BlockSpec(memory_space=pl.ANY)] * len(loaded),
        out_specs=vmem,
        scratch_shapes=[pltpu.VMEM(array.shape, array.dtype) for array in loaded]
        + [block] * 4
        + [lines] * 2
        + [
            pltpu.VMEM((CLOSE, 2 * cells, slots), F32),
            pltpu.VMEM((CLOSE * 4 * cells, slots), BF16),
            pltpu.VMEM((2 * cells, slots), F32),
            pltpu.SemaphoreType.DMA((len(loaded),)),
        ]
        + [one] * 4
        + [halo] * 2,
        compiler_params=pltpu.CompilerParams(
            collective_id=0, has_side_effects=True, vmem_limit_bytes=VMEM_LIMIT
        ),
        cost_estimate=pl.CostEstimate(
            flops=2 * 10**10, bytes_accessed=2 * 10**7, transcendentals=0
        ),
    )(block_count, charges, projection, block_site.reshape(1, slots), near_source, *loaded)


def solution(mesh):
    placed = (
        P(None, None, ("wide", "narrow")),
        P(),
        P(None, ("wide", "narrow"), None, None),
        P(),
        P(("wide", "narrow")),
        P(("wide", "narrow")),
        P(None, ("wide", "narrow")),
    )
    return jax.shard_map(
        per_device,
        mesh=mesh,
        in_specs=placed,
        out_specs=P(None, None, ("wide", "narrow")),
        check_vma=False,
    )
```

```python
import functools

import jax
import jax.numpy as jnp
import ml_dtypes
import numpy as np
from jax import lax
from jax.experimental import pallas as pl
from jax.experimental.pallas import tpu as pltpu
from jax.sharding import PartitionSpec as P

PX = 4
PY = 64
PZ = 128
SPAN_Y = PY // 4
SPAN_Z = PZ // 4
ROW = 2 * PY
WIDTH = PX * ROW
VMEM_LIMIT = 56 * 1024 * 1024
CLOSE = 9
F32 = jnp.float32
BF16 = jnp.bfloat16


def halves(table):
    high = table.astype(np.float32).astype(ml_dtypes.bfloat16)
    low = (table - high.astype(np.float64)).astype(np.float32).astype(ml_dtypes.bfloat16)
    return high, low


def waves(left, right, length):
    angles = 2.0 * np.pi * (np.outer(left, right) % length) / length
    return np.cos(angles), np.sin(angles)


def parts_of(planes):
    return 2 if planes % 8 == 0 else 1


@functools.lru_cache(maxsize=None)
def constant_tables(wide_count, narrow_count):
    whole_x = 2 * PX * wide_count
    whole_y = 2 * PY * narrow_count
    whole_z = 2 * PZ
    ez, ex, part, ey, _ = np.unravel_index(
        np.arange(4 * WIDTH), (4, PX, 2, 4, SPAN_Y)
    )
    owner = part * 64 + 16 * ex + 4 * ey + ez
    spread = (np.arange(128)[:, None] == owner[None, :]).astype(ml_dtypes.bfloat16)
    depth = (4 * np.arange(SPAN_Z)[None, :] + np.arange(4)[:, None]).reshape(-1)
    devices = wide_count * narrow_count
    planes = whole_z // devices
    parts = parts_of(planes)
    order = np.arange(whole_z).reshape(devices, parts, planes // parts)
    order = order.transpose(1, 0, 2).reshape(-1)
    cos_z, sin_z = waves(order, depth, whole_z)
    forward_z = np.concatenate([cos_z, sin_z], axis=1)
    inverse_z = np.concatenate([cos_z.T, sin_z.T], axis=1) / (whole_x * whole_y * whole_z)
    line = (4 * np.arange(SPAN_Y)[None, :] + np.arange(4)[:, None]).reshape(-1)
    points = (PY * np.arange(narrow_count)[:, None] + line[None, :]).reshape(-1)
    cos_y, sin_y = waves(points, np.arange(whole_y), whole_y)
    real_rows = np.concatenate([cos_y, -sin_y], axis=1).reshape(narrow_count, 1, PY, 2 * whole_y)
    imag_rows = np.concatenate([sin_y, cos_y], axis=1).reshape(narrow_count, 1, PY, 2 * whole_y)
    forward_y = np.concatenate([real_rows, imag_rows], axis=1).reshape(-1, 2 * whole_y)
    near_x = (PX * np.arange(wide_count)[None, :] + np.arange(PX)[:, None]).reshape(-1)
    cos_x, sin_x = waves(np.arange(whole_x), near_x, whole_x)
    forward_x = np.block([[cos_x, sin_x], [-sin_x, cos_x]])
    packed = []
    for table in (forward_x, forward_x.T):
        high, low = halves(table)
        packed.append(np.concatenate([high, high, low], axis=1))
    return {
        "spread": spread,
        "gather": np.ascontiguousarray(spread.T),
        "forward_z": halves(forward_z),
        "inverse_z": halves(inverse_z),
        "forward_y": halves(forward_y),
        "inverse_y": halves(np.ascontiguousarray(forward_y.T)),
        "forward_x": packed[0],
        "inverse_x": packed[1],
    }


def split(values):
    high = values.astype(BF16)
    return high, (values - high.astype(F32)).astype(BF16)


def dot(left, right, dims=((1,), (0,))):
    return lax.dot_general(left, right, (dims, ((), ())), preferred_element_type=F32)


def dot3(left, right, dims=((1,), (0,))):
    lh, ll = left
    rh, rl = right
    return dot(lh, rh, dims) + (dot(ll, rh, dims) + dot(lh, rl, dims))


def turned(values, sign):
    lanes = lax.broadcasted_iota(jnp.int32, (values.shape[0], ROW), 1)
    factor = jnp.where(lanes < PY, sign, -sign).astype(F32)
    pieces = [
        pltpu.roll(values[:, i * ROW : (i + 1) * ROW], PY, 1) * factor
        for i in range(values.shape[1] // ROW)
    ]
    return jnp.concatenate(pieces, axis=1)


def columns_of(row, slots):
    return jnp.broadcast_to(row.astype(F32), (128, slots)).T


def own_line(site, slots):
    line = columns_of(site // SPAN_Z, slots)
    lanes = lax.broadcasted_iota(jnp.int32, (slots, 128), 1) % SPAN_Y
    match = line == lanes.astype(F32)
    return jnp.concatenate([match.astype(F32)] * (WIDTH // 128), axis=1)


def place(masked, projection, site, table):
    slots = masked.shape[1]
    cells = masked.shape[0] // 2
    weights = split(projection)
    stencil = jnp.concatenate(
        [dot3(weights, split(masked[r * cells : (r + 1) * cells])) for r in range(2)], axis=0
    ).T
    high, low = split(stencil)
    spread = dot(jnp.concatenate([high, low], axis=1), jnp.concatenate([table, table], axis=0))
    mask = own_line(site, slots)
    depth = lax.broadcasted_iota(jnp.int32, (SPAN_Z, slots), 0)
    picker = (depth == site % SPAN_Z).astype(F32).astype(BF16)
    rows = []
    for ez in range(4):
        high, low = split(spread[:, ez * WIDTH : (ez + 1) * WIDTH] * mask)
        rows.append(dot(picker, high) + dot(picker, low))
    grid = jnp.concatenate(rows, axis=0)
    return jnp.concatenate([grid, turned(grid, 1.0)], axis=0)


def gather_points(grid, site, slots, table):
    mask = own_line(site, slots)
    depth = lax.broadcasted_iota(jnp.int32, (slots, 128), 1)
    match = columns_of(site % SPAN_Z, slots) == depth.astype(F32)
    picker = match.astype(F32).astype(BF16)[:, :SPAN_Z]
    total = jnp.zeros((slots, 128), F32)
    for ez in range(4):
        high, low = split(grid[ez * SPAN_Z : (ez + 1) * SPAN_Z])
        taken = (dot(picker, high) + dot(picker, low)) * mask
        high, low = split(taken)
        rows = table[ez * WIDTH : (ez + 1) * WIDTH, :]
        total = total + (dot(high, rows) + dot(low, rows))
    return total.T


def plane_transforms(z, lines, back, green, fx, ix, wide, group):
    whole_x = green.shape[1]
    half_x = whole_x // 2
    chunks = lines.shape[0]
    rows = [pl.ds(z * PX + ex, wide, stride=group) for ex in range(PX)]
    taken = [
        jnp.concatenate([lines[c, at, :] for at in rows], axis=0) for c in range(chunks)
    ]
    column = jnp.concatenate(
        [
            jnp.concatenate(taken[: chunks // 2], axis=1),
            jnp.concatenate(taken[chunks // 2 :], axis=1),
        ],
        axis=0,
    )
    high, low = split(column)
    freq = dot(fx[...], jnp.concatenate([high, low, high], axis=0))
    real, imag = freq[:whole_x], freq[whole_x:]
    gr, gi = green[0], green[1]
    product = jnp.concatenate([gr * real - gi * imag, gr * imag + gi * real], axis=0)
    high, low = split(product)
    column = dot(ix[...], jnp.concatenate([high, low, high], axis=0))
    for c in range(chunks):
        part, lane = divmod(c, chunks // 2)
        for ex, at in enumerate(rows):
            top = part * half_x + ex * wide
            back[c, at, :] = column[top : top + wide, lane * 128 : (lane + 1) * 128]


def near_prepare(k, source, table, close, onehots, matrices, picked):
    slots = source.shape[1]
    row = source[pl.ds(k, 1), :]
    slot = lax.broadcasted_iota(jnp.int32, (slots, slots), 0)
    onehot = (slot == row % slots).astype(F32).astype(BF16)
    onehots[k] = onehot
    real, imag = table[k, 0], table[k, 1]
    matrix = jnp.concatenate(
        [jnp.concatenate([real, -imag], axis=1), jnp.concatenate([imag, real], axis=1)],
        axis=0,
    )
    high, low = split(matrix)
    matrices[k] = jnp.concatenate([high, high, low], axis=1)
    some = dot(close[CLOSE // 2], onehot)
    picked[k] = jnp.where(row // slots == CLOSE // 2, some, 0.0).astype(BF16)


def near_pick(k, blocks, source, close, onehots, picked):
    slots = source.shape[1]
    block = source[pl.ds(k, 1), :] // slots
    onehot = onehots[k]
    columns = picked[k].astype(F32)
    for i in blocks:
        columns = jnp.where(block == i, dot(close[i], onehot), columns)
    return columns.astype(BF16)


def operator_kernel(wide, narrow, loads, *refs):
    count, charges, projection, site, source = refs[:5]
    far_refs = refs[5 : 5 + loads]
    out = refs[5 + loads]
    held = refs[6 + loads : 6 + 2 * loads]
    (
        send_a, recv_a, send_b, recv_b, lines, back, cube, close, near, onehots, matrices, picked,
        load_sem, send_sem_a, recv_sem_a, send_sem_b, recv_sem_b, halo_send, halo_recv,
    ) = refs[6 + 2 * loads :]
    spread, fzh, fzl, fyh, fyl, fx, green, ix, iyh, iyl, near_table, izh, izl, gather = held
    devices = wide * narrow
    w, n = lax.axis_index("wide"), lax.axis_index("narrow")
    me = w * narrow + n
    _, cells, slots = charges.shape
    planes = green.shape[1]
    chunks = lines.shape[0]
    parts = parts_of(planes)
    part_planes = planes // parts
    group = send_a.shape[1] // devices
    spacing = group // part_planes
    classes = source.shape[0]
    if group > PX * part_planes:
        send_a[...] = jnp.zeros(send_a.shape, F32)
        back[...] = jnp.zeros(back.shape, F32)

    barrier = pltpu.get_barrier_semaphore()

    def place_of(step):
        to = lax.rem(me + step, devices)
        return to, (lax.div(to, narrow), lax.rem(to, narrow))

    def greet(step, carry):
        pl.semaphore_signal(
            barrier, inc=1, device_id=place_of(step)[1], device_id_type=pl.DeviceIdType.MESH
        )
        return carry

    lax.fori_loop(1, devices, greet, 0)
    copies = [
        pltpu.make_async_copy(far_refs[i], held[i], load_sem.at[i]) for i in range(loads)
    ]
    for copy in copies:
        copy.start()

    def rows_of(device):
        return pl.ds(pl.multiple_of(device * group, 8), group)

    def exchange(step, part, send, recv, send_sem, recv_sem):
        to, device = place_of(step)
        return pltpu.make_async_remote_copy(
            src_ref=send.at[part, rows_of(to)],
            dst_ref=recv.at[part, rows_of(me)],
            send_sem=send_sem.at[part, step],
            recv_sem=recv_sem.at[part, step],
            device_id=device,
            device_id_type=pl.DeviceIdType.MESH,
        )

    def start_all(*buffers):
        def one(step, carry):
            exchange(step, *buffers).start()
            return carry

        lax.fori_loop(1, devices, one, 0)

    def receive_all(*buffers):
        def one(step, carry):
            exchange(step, *buffers).wait_recv()
            return carry

        lax.fori_loop(1, devices, one, 0)

    def sent_all(*buffers):
        def one(step, carry):
            exchange(step, *buffers).wait_send()
            return carry

        lax.fori_loop(1, devices, one, 0)

    def beside(index, src, dst, device):
        return pltpu.make_async_remote_copy(
            src_ref=src,
            dst_ref=dst,
            send_sem=halo_send.at[index],
            recv_sem=halo_recv.at[index],
            device_id=device,
            device_id_type=pl.DeviceIdType.MESH,
        )

    narrow_halo = (
        (n < narrow - 1, n > 0, beside(0, cube.at[4], cube.at[3], (w, n + 1))),
        (n > 0, n < narrow - 1, beside(1, cube.at[4], cube.at[5], (w, n - 1))),
    )
    wide_halo = (
        (w < wide - 1, w > 0, beside(2, cube.at[3:6], cube.at[0:3], (w + 1, n))),
        (w > 0, w < wide - 1, beside(3, cube.at[3:6], cube.at[6:9], (w - 1, n))),
    )

    def start_halo(halo):
        for sends, _, copy in halo:
            pl.when(sends)(copy.start)

    def receive_halo(halo):
        for _, receives, copy in halo:
            pl.when(receives)(copy.wait_recv)

    def sent_halo(halo):
        for sends, _, copy in halo:
            pl.when(sends)(copy.wait_send)

    for outside, blocks in (
        (n == 0, (3, 4)),
        (n == narrow - 1, (5, 6)),
        (w == 0, (0, 3)),
        (w == wide - 1, (6, 9)),
    ):

        @pl.when(outside)
        def _(blocks=blocks):
            for i in range(*blocks):
                cube[i] = jnp.zeros(cube.shape[1:], F32)

    slot = lax.broadcasted_iota(jnp.int32, (1, slots), 1)
    occupied = (slot < count[0]).astype(F32)
    masked = jnp.concatenate([charges[r] * occupied for r in range(2)], axis=0)
    cube[4] = masked
    copies[0].wait()
    grid = place(masked, projection[...], site[...], spread[...])
    copies[1].wait()
    copies[2].wait()
    freq = dot3((fzh[...], fzl[...]), split(grid))
    some = devices * part_planes
    for p in range(parts):
        for ex in range(PX):
            send_a[p, pl.ds(ex, some, stride=spacing), :] = freq[
                p * some : (p + 1) * some, ex * ROW : (ex + 1) * ROW
            ]

    first = (send_a, recv_a, send_sem_a, recv_sem_a)
    second = (send_b, recv_b, send_sem_b, recv_sem_b)
    pl.semaphore_wait(barrier, devices - 1)
    start_all(0, *first)
    start_halo(narrow_halo)
    for p in range(1, parts):
        start_all(p, *first)
    for p in range(parts):
        recv_a[p, rows_of(me), :] = send_a[p, rows_of(me), :]

    def own_copy(i):
        high, low = split(cube[i])
        close[i] = jnp.concatenate([high, low], axis=0)

    def each_class(body):
        def three(j, carry):
            for u in range(3):
                body(3 * j + u)
            return carry

        lax.fori_loop(0, classes // 3, three, 0)
        for k in range(classes - classes % 3, classes):
            body(k)

    own_copy(4)
    near[...] = jnp.zeros(near.shape, F32)
    for copy in copies[3:]:
        copy.wait()
    each_class(
        lambda k: near_prepare(k, source, near_table, close, onehots, matrices, picked)
    )

    def part_transforms(p):
        values = recv_a[p].reshape(wide, narrow, group, ROW)
        field = jnp.concatenate(
            [values[:, i].reshape(wide * group, ROW) for i in range(narrow)], axis=1
        )
        freq = dot3(split(field), (fyh[...], fyl[...]))
        for c in range(chunks):
            lines[c] = freq[:, c * 128 : (c + 1) * 128]
        for z in range(part_planes):
            plane_transforms(
                z, lines, back, green[:, p * part_planes + z], fx, ix, wide, group
            )
        field = jnp.concatenate([back[c] for c in range(chunks)], axis=1)
        result = dot3(split(field), (iyh[...], iyl[...]))
        for i in range(narrow):
            for j in range(wide):
                top = (j * narrow + i) * group
                send_b[p, top : top + group, :] = result[
                    j * group : (j + 1) * group, i * ROW : (i + 1) * ROW
                ]
        start_all(p, *second)
        recv_b[p, rows_of(me), :] = send_b[p, rows_of(me), :]

    for p in range(parts):
        receive_all(p, *first)
        part_transforms(p)
        if p == 0:
            receive_halo(narrow_halo)
            start_halo(wide_halo)
            own_copy(3)
            own_copy(5)

            def narrow_class(k):
                picked[k] = near_pick(k, (3, 5), source, close, onehots, picked)

            each_class(narrow_class)

    receive_halo(wide_halo)
    others = (0, 1, 2, 6, 7, 8)
    for i in others:
        own_copy(i)

    def wide_class(k):
        columns = near_pick(k, others, source, close, onehots, picked)
        columns = jnp.concatenate([columns, columns[: 2 * cells]], axis=0)
        near[...] += dot(matrices[k], columns)

    each_class(wide_class)

    for p in range(parts):
        receive_all(p, *second)
    freq = jnp.concatenate(
        [
            jnp.concatenate(
                [recv_b[p, pl.ds(ex, some, stride=spacing), :] for p in range(parts)], axis=0
            )
            for ex in range(PX)
        ],
        axis=1,
    )
    both = jnp.concatenate([freq, turned(freq, -1.0)], axis=0)
    grid = dot3((izh[...], izl[...]), split(both))
    taken = gather_points(grid, site[...], slots, gather)
    weights = split(projection[...])
    for r in range(2):
        far = dot3(weights, split(taken[r * 64 : (r + 1) * 64]), ((0,), (0,)))
        out[r] = (far + near[r * cells : (r + 1) * cells, :]) * occupied
    for p in range(parts):
        sent_all(p, *first)
        sent_all(p, *second)
    sent_halo(narrow_halo)
    sent_halo(wide_halo)


def per_device(charges, projection, green_hat, near_table, block_site, block_count, near_source):
    wide = lax.axis_size("wide")
    narrow = lax.axis_size("narrow")
    devices = wide * narrow
    tables = constant_tables(wide, narrow)
    cells, slots = charges.shape[1:]
    planes = green_hat.shape[1]
    whole_x, whole_y = green_hat.shape[2:]
    loaded = (
        tables["spread"],
        *tables["forward_z"],
        *tables["forward_y"],
        tables["forward_x"],
        green_hat,
        tables["inverse_x"],
        *tables["inverse_y"],
        near_table,
        *tables["inverse_z"],
        tables["gather"],
    )
    parts = parts_of(planes)
    group = max(8, PX * planes // parts)
    classes = near_source.shape[0]
    block = pltpu.VMEM((parts, devices * group, ROW), F32)
    lines = pltpu.VMEM((2 * whole_y // 128, wide * group, 128), F32)
    one = pltpu.SemaphoreType.DMA((parts, devices))
    halo = pltpu.SemaphoreType.DMA((4,))
    vmem = pl.BlockSpec(memory_space=pltpu.VMEM)
    return pl.pallas_call(
        functools.partial(operator_kernel, wide, narrow, len(loaded)),
        out_shape=jax.ShapeDtypeStruct((2, cells, slots), F32),
        in_specs=[pl.BlockSpec(memory_space=pltpu.SMEM)]
        + [vmem] * 4
        + [pl.BlockSpec(memory_space=pl.ANY)] * len(loaded),
        out_specs=vmem,
        scratch_shapes=[pltpu.VMEM(array.shape, array.dtype) for array in loaded]
        + [block] * 4
        + [lines] * 2
        + [
            pltpu.VMEM((CLOSE, 2 * cells, slots), F32),
            pltpu.VMEM((CLOSE, 4 * cells, slots), BF16),
            pltpu.VMEM((2 * cells, slots), F32),
            pltpu.VMEM((classes, slots, slots), BF16),
            pltpu.VMEM((classes, 2 * cells, 6 * cells), BF16),
            pltpu.VMEM((classes, 4 * cells, slots), BF16),
            pltpu.SemaphoreType.DMA((len(loaded),)),
        ]
        + [one] * 4
        + [halo] * 2,
        compiler_params=pltpu.CompilerParams(
            collective_id=0, has_side_effects=True, vmem_limit_bytes=VMEM_LIMIT
        ),
        cost_estimate=pl.CostEstimate(
            flops=2 * 10**10, bytes_accessed=2 * 10**7, transcendentals=0
        ),
    )(block_count, charges, projection, block_site.reshape(1, slots), near_source, *loaded)


def solution(mesh):
    placed = (
        P(None, None, ("wide", "narrow")),
        P(),
        P(None, ("wide", "narrow"), None, None),
        P(),
        P(("wide", "narrow")),
        P(("wide", "narrow")),
        P(None, ("wide", "narrow")),
    )
    return jax.shard_map(
        per_device,
        mesh=mesh,
        in_specs=placed,
        out_specs=P(None, None, ("wide", "narrow")),
        check_vma=False,
    )
```
